128 devices in a mesh: cells: 128 (over y, z, x, core).
Axes of the slice: x: 4, y: 4, z: 4, core: 2. Of those that a mesh axis runs over, the one named last changes fastest.
Arguments:
- source_cells: bfloat16 [5120, 50, 256], P('cells')
- target_cells: bfloat16 [5120, 50, 256], P('cells')
- partners: int32 [5120, 6], P('cells'), may hold values from -1 to 5119, as said below
- home: int32 [5120], replicated, may hold values from 0 to 5119, as said below
Outputs:
- source_potential: float32 [5120, 256], P('cells')
- target_potential: float32 [5120, 256], P('cells')
The draws below stay inside these ranges and needn't reach their ends.
Inputs may be any that keep to these rules, and one draw needn't show every extreme that they name: `home`: A permutation of the cluster ids. `partners`: in each row the ids come first and the -1 entries after them; the first entry is never -1; ids in a row are distinct; every target cluster id appears in some row; the slot of each listed id lies on the device of the source cluster or on one of its two neighbours along cells, cyclically (slot // 40 differs by -1, 0 or 1 modulo the number of devices); some row has all 6 entries set.
All inputs are finite; a program needn't handle non-finite values.
Results may differ from the reference program's by a relative error of at most 0.0014.
Values may be sent and summed in bfloat16 or wider, within the bound.
A program may use at most 64 MiB of HBM per device.

```python
import jax
import jax.numpy as jnp
from jax import lax

P_SIZE = 50
CS = 256
CPD = 40
MAXP = 6
ITERS = 2
NC = 5120
N_CELLS = 128


def pair_tables(key):
    order = jax.random.permutation(jax.random.fold_in(key, 101), NC).astype(jnp.int32)
    named = jnp.argsort(order).astype(jnp.int32)
    slot = jnp.arange(NC, dtype=jnp.int32)
    device = slot // CPD
    limit = jax.random.randint(jax.random.fold_in(key, 102), (N_CELLS,), 1, MAXP + 1).astype(jnp.int32)
    limit = limit.at[0].set(MAXP)
    count = jax.random.randint(jax.random.fold_in(key, 103), (NC,), 1, limit[device] + 1).astype(jnp.int32)
    count = count.at[0].set(MAXP)
    span = 3 * CPD
    score = jax.random.randint(jax.random.fold_in(key, 104), (NC, span), 0, 65536).astype(jnp.int32) * span + jnp.arange(span, dtype=jnp.int32)[None, :]
    own = CPD + slot % CPD
    score = jnp.where(jnp.arange(span, dtype=jnp.int32)[None, :] == own[:, None], -1, score)
    _, picked = lax.top_k(score, MAXP - 1)
    chosen = jnp.concatenate([own[:, None], picked.astype(jnp.int32)], axis=1)
    target_slot = jnp.mod((device[:, None] - 1) * CPD + chosen, NC).astype(jnp.int32)
    used = jnp.arange(MAXP, dtype=jnp.int32)[None, :] < count[:, None]
    listed = jnp.where(used, named[target_slot], -1).astype(jnp.int32)
    return (order, listed)


def draw_home(key, part):
    return pair_tables(key)[0]


def draw_partners(key, part):
    return pair_tables(key)[1]


def draw_source_cells(key, part):
    key = jax.random.fold_in(key, 7)
    centre = jax.random.normal(jax.random.fold_in(key, 1), (NC, P_SIZE, 1), jnp.float32) * 0.3
    spread = jax.random.normal(jax.random.fold_in(key, 2), (NC, P_SIZE, CS), jnp.float32) * 0.25
    return (centre + spread).astype(jnp.bfloat16)


def draw_target_cells(key, part):
    key = jax.random.fold_in(key, 8)
    centre = jax.random.normal(jax.random.fold_in(key, 1), (NC, P_SIZE, 1), jnp.float32) * 0.3
    spread = jax.random.normal(jax.random.fold_in(key, 2), (NC, P_SIZE, CS), jnp.float32) * 0.25
    return (centre + spread).astype(jnp.bfloat16)


def setup_inputs(seed: int = 0) -> dict:
    arg_keys = jax.random.split(jax.random.key(seed), 5)
    source_cells = draw_source_cells(jax.random.fold_in(arg_keys[4], 71), 0)
    target_cells = draw_target_cells(jax.random.fold_in(arg_keys[4], 71), 0)
    partners = draw_partners(jax.random.fold_in(arg_keys[4], 71), 0)
    home = draw_home(jax.random.fold_in(arg_keys[4], 71), 0)
    return dict(source_cells=source_cells, target_cells=target_cells, partners=partners, home=home)


entropy = 0.5


def reference(source_cells, target_cells, partners, home):
    total_cells = NC * CS
    offset = entropy * jnp.log(jnp.float32(total_cells))
    source_wide = source_cells.astype(jnp.float32)
    target_wide = target_cells.astype(jnp.float32)
    source_sq = jnp.sum(source_wide * source_wide, axis=1)
    target_sq = jnp.sum(target_wide * target_wide, axis=1)
    valid = partners >= 0
    slot = jnp.where(valid, home[jnp.maximum(partners, 0)], 0).astype(jnp.int32)
    segment = jnp.where(valid, slot, NC).reshape(-1).astype(jnp.int32)

    def iterate(source_pot, target_pot):
        def one(carry, inputs):
            feats, squares, pot, rows, live = inputs
            blocks = target_wide[rows]
            cross = jnp.einsum('pi,kpj->kij', feats.astype(jnp.float32), blocks)
            cost = 0.5 * (squares[None, :, None] + target_sq[rows][:, None, :]) - cross
            row_logit = (target_pot[rows][:, None, :] - cost) / entropy
            row_logit = jnp.where(live[:, None, None], row_logit, -jnp.inf)
            top = jnp.max(row_logit, axis=(0, 2))
            row_lse = top + jnp.log(jnp.sum(jnp.exp(row_logit - top[None, :, None]), axis=(0, 2)))
            col_logit = (pot[None, :, None] - cost) / entropy
            col_top = jnp.max(col_logit, axis=1)
            col_lse = col_top + jnp.log(jnp.sum(jnp.exp(col_logit - col_top[:, None, :]), axis=1))
            return carry, (row_lse, col_lse)

        start = jnp.zeros((), jnp.float32)
        _, (row_lse, col_lse) = lax.scan(one, start, (source_cells, source_sq, source_pot, slot, valid))
        flat = col_lse.reshape(NC * MAXP, CS)
        peak = jax.ops.segment_max(flat, segment, num_segments=NC + 1)
        mass = jax.ops.segment_sum(jnp.exp(flat - peak[segment]), segment, num_segments=NC + 1)
        col_total = (peak + jnp.log(mass))[:NC]
        source_new = -entropy * row_lse + offset
        target_new = -entropy * col_total + offset
        return 0.5 * (source_pot + source_new), 0.5 * (target_pot + target_new)

    source_pot = jnp.zeros((NC, CS), jnp.float32)
    target_pot = jnp.zeros((NC, CS), jnp.float32)
    for step in range(ITERS):
        source_pot, target_pot = iterate(source_pot, target_pot)
    return source_pot, target_pot
```

```python
import functools
import math

import jax
import jax.numpy as jnp
from jax import lax
from jax.experimental import pallas as pl
from jax.experimental.pallas import tpu as pltpu
from jax.sharding import PartitionSpec as P

F32 = jnp.float32
BF16 = jnp.bfloat16
entropy = 0.5
SHIFT = 48.0
SQ_LIMIT = 24.0
G_SHIFT = 24.0
NEVER = -1e30
WAYS = 2
MANY = 8
DEPTH = 64
REGION = 256
COUNTS = 3 * REGION

VMEM = pl.BlockSpec(memory_space=pltpu.VMEM)
HBM = pl.BlockSpec(memory_space=pltpu.HBM)
SMEM = pl.BlockSpec(memory_space=pltpu.SMEM)


def row_of(index, shape):
    return lax.broadcasted_iota(jnp.int32, shape, 0) == index


def pieces(x):
    high = x.astype(BF16).astype(F32)
    middle = (x - high).astype(BF16).astype(F32)
    low = (x - high - middle).astype(BF16).astype(F32)
    return high, middle, low


def extend(wide, first, second):
    last = wide[48:56]
    for at, value in enumerate(first + second):
        last = jnp.where(row_of(at + 2, last.shape), value, last)
    return jnp.concatenate([wide[:48], last, jnp.zeros_like(last)], axis=0)


def widen(block_ref, wide_ref):
    depth, blocks, _ = block_ref.shape

    def turn(p, carry):
        full = block_ref[p].astype(F32)
        for half in range(2):
            wide_ref[half, pl.ds(p * blocks, blocks)] = full[:, half * 128 : half * 128 + 128]
        return carry

    lax.fori_loop(0, depth, turn, 0, unroll=5)
    rest = (56 - depth) * blocks
    for half in range(2):
        wide_ref[half, pl.ds(depth * blocks, rest)] = jnp.zeros((rest, 128), F32)


def cluster(wide_ref, blocks, slot):
    halves = [wide_ref[half, pl.ds(slot, 56, stride=blocks)] for half in range(2)]
    return jnp.concatenate(halves, axis=1)


def prepare_target(wide, slot, base, out_ref, top):
    square = jnp.sum(wide * wide, axis=0, keepdims=True)
    out_ref[base + slot] = extend(wide, pieces(-square), (1.0, 1.0, 1.0)).astype(BF16)
    return jnp.maximum(top, square)


def prepare_source(wide, slot, out_ref, top):
    square = jnp.sum(wide * wide, axis=0, keepdims=True)
    full = extend(2.0 * wide, (1.0, 1.0, 1.0), pieces(SHIFT - square))
    out_ref[slot] = full.T.astype(BF16)
    return jnp.maximum(top, square)


def entry(lists_ref, at):
    code = lists_ref[at]
    return code // 128, lax.rem(code, 128)


def base_of(lists_ref, region):
    base = 0
    for r in range(region):
        base = base + lists_ref[COUNTS + r]
    return base


def in_groups(count, pair):
    def turn(start, ways):
        def body(step, carry):
            for way in range(ways):
                pair(start + step * ways + way)
            return carry

        return body

    groups = count // MANY
    lax.fori_loop(0, groups, turn(0, MANY), 0)
    rest = count - groups * MANY
    lax.fori_loop(0, rest // WAYS, turn(groups * MANY, WAYS), 0)


def first_sweep(region, lists_ref, at_ref, b_ref, k_ref, rows_ref, cols_ref):
    base = base_of(lists_ref, region)

    def pair(at):
        s, w = entry(lists_ref, region * REGION + at)
        logit = jnp.dot(at_ref[s], b_ref[w], preferred_element_type=F32)
        weight = jnp.exp(logit)
        k_ref[base + at] = weight.astype(BF16)
        rows_ref[s] += weight[:, :128] + weight[:, 128:]
        cols_ref[pl.ds(w, 1)] += jnp.sum(weight, axis=0, keepdims=True)

    in_groups(lists_ref[COUNTS + region], pair)


def prepare_kernel(
    source_in, target_in, partners_in, home_in,
    at_ref, b_ref, lists_ref, top_ref,
    source_ref, target_ref, partners_ref, home_ref, sems, source_wide, target_wide,
):
    loads = [
        pltpu.make_async_copy(given, held, sems.at[i])
        for i, (given, held) in enumerate((
            (partners_in, partners_ref), (home_in, home_ref),
            (source_in, source_ref), (target_in, target_ref),
        ))
    ]
    for load in loads:
        load.start()
    for load in loads:
        load.wait()
    links, blocks = partners_ref.shape
    clusters = home_ref.shape[0]
    here = lax.axis_index("cells")
    sibling = 2 - 2 * lax.rem(here, 2)
    cells = source_ref.shape[2]
    widen(source_ref, source_wide)
    widen(target_ref, target_wide)

    def turn(s, carry):
        counts, top = carry
        for m in range(links):
            name = partners_ref[m, s]
            live = name >= 0
            slot = home_ref[jnp.maximum(name, 0)]
            w = slot - (here - 1) * blocks
            w = jnp.where(w < 0, w + clusters, w)
            w = jnp.where(w >= clusters, w - clusters, w)
            block = w // blocks
            region = jnp.where(block == 1, 0, jnp.where(block == sibling, 1, 2))
            region = jnp.where(live, region, 3)
            count = jnp.where(
                region == 0, counts[0], jnp.where(region == 1, counts[1], counts[2])
            )
            place = jnp.where(live, region * REGION + count, COUNTS + 8)
            lists_ref[place] = s * 128 + w
            counts = tuple(c + jnp.where(region == r, 1, 0) for r, c in enumerate(counts))
        top = prepare_source(cluster(source_wide, blocks, s), s, at_ref, top)
        top = prepare_target(cluster(target_wide, blocks, s), s, blocks, b_ref, top)
        return counts, top

    zero = jnp.int32(0)
    counts, top = lax.fori_loop(
        0, blocks, turn, ((zero, zero, zero), jnp.zeros((1, cells), F32)), unroll=4
    )
    dummy = 3 * blocks
    for r, count in enumerate(counts):
        for extra in range(WAYS - 1):
            lists_ref[r * REGION + count + extra] = dummy
        lists_ref[COUNTS + r] = (count + WAYS - 1) // WAYS * WAYS
    shape = b_ref.shape[1:]
    b_ref[dummy] = jnp.where(row_of(50, shape), NEVER, 0.0).astype(BF16)
    top_ref[...] = jnp.broadcast_to(top, top_ref.shape)


def take_block(which, block_ref, b_ref, top_ref, stage_ref, sem, wide_ref):
    blocks = block_ref.shape[1]
    load = pltpu.make_async_copy(block_ref, stage_ref, sem)
    load.start()
    load.wait()
    widen(stage_ref, wide_ref)
    here = lax.axis_index("cells")
    side = 2 - 2 * lax.rem(here, 2)
    base = (side if which == 1 else 2 - side) * blocks

    def turn(t, top):
        return prepare_target(cluster(wide_ref, blocks, t), t, base, b_ref, top)

    top = lax.fori_loop(0, blocks, turn, top_ref[0:1], unroll=4)
    top_ref[...] = jnp.broadcast_to(top, top_ref.shape)


def within(top_ref):
    return jnp.max(top_ref[0:1]) <= SQ_LIMIT


def near_kernel(
    block_ref, at_ref, lists_ref, b_in, top_in,
    b_ref, top_ref, k_ref, rows_ref, cols_ref, stage_ref, sem, wide_ref,
):
    cols_ref[...] = jnp.zeros(cols_ref.shape, F32)

    def start(s, carry):
        rows_ref[s] = jnp.zeros(rows_ref.shape[1:], F32)
        return carry

    lax.fori_loop(0, rows_ref.shape[0], start, 0, unroll=4)
    take_block(1, block_ref, b_ref, top_ref, stage_ref, sem, wide_ref)
    first_sweep(0, lists_ref, at_ref, b_ref, k_ref, rows_ref, cols_ref)
    first_sweep(1, lists_ref, at_ref, b_ref, k_ref, rows_ref, cols_ref)


def each_pair(lists_ref, body):
    for region in range(3):

        def turn(at, carry, region=region):
            body(*entry(lists_ref, region * REGION + at))
            return carry

        lax.fori_loop(0, lists_ref[COUNTS + region], turn, 0)


def careful_rows(lists_ref, at_ref, b_ref, rows_ref, weight_row, out_ref, log_n):
    shape = rows_ref.shape[1:]
    left = lax.broadcasted_iota(jnp.int32, shape, 1) < 64

    def start(s, carry):
        rows_ref[s] = jnp.where(left, NEVER, 0.0)
        return carry

    lax.fori_loop(0, rows_ref.shape[0], start, 0)

    def body(s, w):
        logit = jnp.dot(at_ref[s], b_ref[w], preferred_element_type=F32) + weight_row(w)
        held = rows_ref[s]
        top, total = held[:, 0:1], held[:, 64:65]
        new_top = jnp.maximum(top, jnp.max(logit, axis=1, keepdims=True))
        total = total * jnp.exp(top - new_top)
        total = total + jnp.sum(jnp.exp(logit - new_top), axis=1, keepdims=True)
        rows_ref[s] = jnp.where(left, new_top, total)

    each_pair(lists_ref, body)

    def finish(s, carry):
        held = rows_ref[s]
        lse = held[:, 0:1] + jnp.log(held[:, 64:65]) - SHIFT
        wide = jnp.broadcast_to(lse, shape)
        out_ref[pl.ds(s, 1)] = wide.T[0:1]
        rows_ref[s] = 0.5 * (log_n - wide)
        return carry

    lax.fori_loop(0, rows_ref.shape[0], finish, 0)


def careful_cols(lists_ref, at_ref, b_ref, weight_col, total_ref, out_ref):
    out_ref[...] = jnp.full(out_ref.shape, NEVER, F32)
    total_ref[...] = jnp.zeros(total_ref.shape, F32)

    def body(s, w):
        logit = jnp.dot(at_ref[s], b_ref[w], preferred_element_type=F32)
        logit = logit - SHIFT + weight_col(s)
        at = pl.ds(w, 1)
        top = out_ref[at]
        new_top = jnp.maximum(top, jnp.max(logit, axis=0, keepdims=True))
        total = total_ref[at] * jnp.exp(top - new_top)
        total_ref[at] = total + jnp.sum(jnp.exp(logit - new_top), axis=0, keepdims=True)
        out_ref[at] = new_top

    each_pair(lists_ref, body)
    total = total_ref[...]
    out_ref[...] = jnp.where(
        total > 0.0, out_ref[...] + jnp.log(jnp.maximum(total, 1e-37)), NEVER
    )


def far_kernel(
    log_n,
    block_ref, at_ref, lists_ref, b_in, top_in, k_in, rows_in, cols_in,
    b_ref, top_ref, k_ref, rows_ref, cols_ref, u_ref, row_lse_ref, col_lse_ref, stage_ref, sem, wide_ref,
):
    take_block(2, block_ref, b_ref, top_ref, stage_ref, sem, wide_ref)
    first_sweep(2, lists_ref, at_ref, b_ref, k_ref, rows_ref, cols_ref)
    fine = within(top_ref)

    @pl.when(fine)
    def _():
        total = cols_ref[...]
        col_lse_ref[...] = jnp.where(
            total > 0.0, jnp.log(jnp.maximum(total, 1e-37)) - SHIFT, NEVER
        )
        ones = jnp.ones((128, 128), BF16)

        def turn(s, carry):
            held = rows_ref[s].astype(BF16)
            wide = jnp.dot(held, ones, preferred_element_type=F32)
            u_ref[s] = lax.rsqrt(wide).astype(BF16)
            line = lax.dot_general(
                ones[0:16], held, (((1,), (1,)), ((), ())), preferred_element_type=F32
            )
            row_lse_ref[pl.ds(s, 1)] = jnp.log(line[0:1]) - SHIFT
            return carry

        lax.fori_loop(0, rows_ref.shape[0], turn, 0, unroll=4)

    @pl.when(jnp.logical_not(fine))
    def _():
        careful_rows(lists_ref, at_ref, b_ref, rows_ref, lambda w: 0.0, row_lse_ref, log_n)
        careful_cols(lists_ref, at_ref, b_ref, lambda s: 0.0, cols_ref, col_lse_ref)


def column_kernel(
    log_n,
    at_ref, lists_ref, b_ref, top_ref, k_ref, rows_ref, u_ref,
    col_lse_ref, cols_ref,
):
    fine = within(top_ref)

    @pl.when(fine)
    def _():
        cols_ref[...] = jnp.zeros(cols_ref.shape, F32)
        for region in range(3):
            base = base_of(lists_ref, region)

            def pair(at, region=region, base=base):
                s, w = entry(lists_ref, region * REGION + at)
                half = u_ref[s]
                part = k_ref[base + at] * jnp.concatenate([half, half], axis=1)
                while part.shape[0] > 16:
                    mid = part.shape[0] // 2
                    part = part[:mid] + part[mid:]
                cols_ref[pl.ds(w, 1)] += jnp.sum(part.astype(F32), axis=0, keepdims=True)

            in_groups(lists_ref[COUNTS + region], pair)
        total = cols_ref[...]
        col_lse_ref[...] = jnp.where(
            total > 0.0,
            jnp.log(jnp.maximum(total, 1e-37)) + (0.5 * log_n - 0.5 * SHIFT),
            NEVER,
        )

    @pl.when(jnp.logical_not(fine))
    def _():
        careful_cols(
            lists_ref, at_ref, b_ref, lambda s: rows_ref[s][:, 0:1], cols_ref, col_lse_ref
        )


def lse_of(values):
    top = functools.reduce(jnp.maximum, values)
    return top + jnp.log(sum(jnp.exp(v - top) for v in values))


def row_kernel(
    log_n,
    at_ref, lists_ref, b_ref, top_ref, k_ref, row_lse_ref, col_lse_ref,
    right_ref, left_ref, right2_ref, left2_ref, rows_in,
    source_ref, own_ref, rows_ref, g_ref, v_ref, second_ref, sums_ref,
):
    blocks = source_ref.shape[0]
    own = col_lse_ref[pl.ds(blocks, blocks)]
    own = lse_of([own, right_ref[pl.ds(0, blocks)], left_ref[pl.ds(blocks, blocks)]])
    low = lse_of([col_lse_ref[pl.ds(0, blocks)], left_ref[pl.ds(0, blocks)], left2_ref[...]])
    high = lse_of(
        [col_lse_ref[pl.ds(2 * blocks, blocks)], right_ref[pl.ds(blocks, blocks)], right2_ref[...]]
    )
    own_g = 0.5 * (log_n - own)
    own_ref[...] = own_g
    g_ref[...] = jnp.zeros(g_ref.shape, F32)
    g_ref[pl.ds(0, blocks)] = 0.5 * (log_n - low)
    g_ref[pl.ds(blocks, blocks)] = own_g
    g_ref[pl.ds(2 * blocks, blocks)] = 0.5 * (log_n - high)
    g = g_ref[...]
    fine = within(top_ref) & (jnp.max(g) <= 60.0) & (jnp.min(g) >= 0.0)

    @pl.when(fine)
    def _():
        v_ref[...] = jnp.exp(g_ref[...] - G_SHIFT)

        def start(s, carry):
            sums_ref[s] = jnp.zeros(sums_ref.shape[1:], BF16)
            return carry

        lax.fori_loop(0, blocks, start, 0, unroll=4)
        for region in range(3):
            base = base_of(lists_ref, region)

            def pair(at, region=region, base=base):
                s, w = entry(lists_ref, region * REGION + at)
                line = jnp.broadcast_to(v_ref[pl.ds(w, 1)].astype(BF16), (256, 256))
                part = k_ref[base + at] * line
                sums_ref[s] += part[:, :128] + part[:, 128:]

            in_groups(lists_ref[COUNTS + region], pair)
        ones = jnp.ones((16, 128), BF16)

        def turn(s, carry):
            line = lax.dot_general(
                ones, sums_ref[s], (((1,), (1,)), ((), ())),
                preferred_element_type=F32,
            )
            second_ref[pl.ds(s, 1)] = jnp.log(line[0:1]) - SHIFT + G_SHIFT
            return carry

        lax.fori_loop(0, blocks, turn, 0, unroll=4)

    @pl.when(jnp.logical_not(fine))
    def _():
        careful_rows(
            lists_ref, at_ref, b_ref, rows_ref, lambda w: g_ref[pl.ds(w, 1)], second_ref, log_n
        )

    first = 0.5 * (log_n - row_lse_ref[...])
    source_ref[...] = (0.5 * entropy) * (first + log_n - second_ref[...])


def in_hbm(array):
    return pltpu.with_memory_space_constraint(array, pltpu.HBM)


def on_device(source_cells, target_cells, partners, home):
    blocks, _, cells = source_cells.shape
    source_cells = source_cells.transpose(1, 0, 2)
    target_cells = target_cells.transpose(1, 0, 2)
    stage = pltpu.VMEM(source_cells.shape, BF16)
    wide = pltpu.VMEM((2, 56 * blocks, 128), F32)
    links = partners.shape[1]
    devices = lax.axis_size("cells")
    log_n = math.log(blocks * devices * cells)
    window = 128
    places = blocks * links + 3 * (WAYS - 1)

    def moved(block, step):
        return lax.ppermute(block, "cells", [(i, step(i) % devices) for i in range(devices)])

    far = in_hbm(moved(target_cells, lambda i: i + 1 if i % 2 else i - 1))
    sibling = in_hbm(moved(target_cells, lambda i: i ^ 1))

    vm = lambda shape, dtype: pltpu.VMEM(shape, dtype)
    at_s = vm((blocks, cells, DEPTH), BF16)
    b_s = vm((3 * blocks + 1, DEPTH, cells), BF16)
    top_s = vm((8, cells), F32)
    k_s = vm((places, cells, cells), BF16)
    rows_s = vm((blocks, cells, 128), F32)
    cols_s = vm((window, cells), F32)
    u_s = vm((blocks, cells, 128), BF16)
    lines_s = vm((blocks, cells), F32)
    limit = pltpu.CompilerParams(vmem_limit_bytes=8 * 2**20)

    at, b, lists, top = pl.pallas_call(
        prepare_kernel,
        out_shape=[at_s, b_s, jax.ShapeDtypeStruct((COUNTS + 16,), jnp.int32), top_s],
        in_specs=[HBM] * 4,
        out_specs=[VMEM, VMEM, SMEM, VMEM],
        scratch_shapes=[
            stage, stage, pltpu.SMEM((links, blocks), jnp.int32), pltpu.SMEM(home.shape, jnp.int32),
            pltpu.SemaphoreType.DMA((4,)), wide, wide,
        ],
        compiler_params=limit,
        name="prepare",
    )(*map(in_hbm, (source_cells, target_cells, partners.T, home)))
    b, top, k, rows, cols = pl.pallas_call(
        near_kernel,
        out_shape=[b_s, top_s, k_s, rows_s, cols_s],
        in_specs=[HBM, VMEM, SMEM, VMEM, VMEM],
        out_specs=[VMEM] * 5,
        input_output_aliases={3: 0, 4: 1},
        scratch_shapes=[stage, pltpu.SemaphoreType.DMA, wide],
        compiler_params=limit,
        name="near_pairs",
    )(sibling, at, lists, b, top)
    b, top, k, rows, cols, u, row_lse, col_lse = pl.pallas_call(
        functools.partial(far_kernel, log_n),
        out_shape=[b_s, top_s, k_s, rows_s, cols_s, u_s, lines_s, cols_s],
        in_specs=[HBM, VMEM, SMEM] + [VMEM] * 5,
        out_specs=[VMEM] * 8,
        input_output_aliases={3: 0, 4: 1, 5: 2, 6: 3, 7: 4},
        scratch_shapes=[stage, pltpu.SemaphoreType.DMA, wide],
        compiler_params=limit,
        name="far_pairs",
    )(far, at, lists, b, top, k, rows, cols)

    right = moved(col_lse[: 2 * blocks], lambda i: i - 1)
    left = moved(col_lse[blocks : 3 * blocks], lambda i: i + 1)
    right2 = moved(col_lse[:blocks], lambda i: i - 2)
    left2 = moved(col_lse[2 * blocks : 3 * blocks], lambda i: i + 2)

    col_lse2, _ = pl.pallas_call(
        functools.partial(column_kernel, log_n),
        out_shape=[cols_s, cols_s],
        in_specs=[VMEM, SMEM] + [VMEM] * 5,
        out_specs=[VMEM] * 2,
        compiler_params=limit,
        name="second_columns",
    )(at, lists, b, top, k, rows, u)
    from_right = moved(col_lse2[:blocks], lambda i: i - 1)
    from_left = moved(col_lse2[2 * blocks : 3 * blocks], lambda i: i + 1)

    source_pot, own_g, *_ = pl.pallas_call(
        functools.partial(row_kernel, log_n),
        out_shape=[lines_s, lines_s, rows_s, cols_s, cols_s, lines_s, u_s],
        in_specs=[VMEM, SMEM] + [VMEM] * 10,
        out_specs=[VMEM] * 7,
        input_output_aliases={11: 2},
        compiler_params=limit,
        name="second_rows",
    )(at, lists, b, top, k, row_lse, col_lse, right, left, right2, left2, rows)

    total = lse_of([col_lse2[blocks : 2 * blocks], from_right, from_left])
    target_pot = (0.5 * entropy) * (own_g + log_n - total)
    return source_pot, target_pot


def solution(mesh):
    in_specs = (P("cells", None, None), P("cells", None, None), P("cells", None), P())
    out_specs = (P("cells", None), P("cells", None))
    return jax.shard_map(
        on_device, mesh=mesh, in_specs=in_specs, out_specs=out_specs, check_vma=False
    )
```

```python
import functools
import math

import jax
import jax.numpy as jnp
from jax import lax
from jax.experimental import pallas as pl
from jax.experimental.pallas import tpu as pltpu
from jax.sharding import PartitionSpec as P

F32 = jnp.float32
BF16 = jnp.bfloat16
entropy = 0.5
SHIFT = 48.0
SQ_LIMIT = 24.0
G_SHIFT = 24.0
NEVER = -1e30
WAYS = 2
MANY = 16
DEPTH = 64
REGION = 256
COUNTS = 3 * REGION

VMEM = pl.BlockSpec(memory_space=pltpu.VMEM)
HBM = pl.BlockSpec(memory_space=pltpu.HBM)
SMEM = pl.BlockSpec(memory_space=pltpu.SMEM)


def row_of(index, shape):
    return lax.broadcasted_iota(jnp.int32, shape, 0) == index


def pieces(x):
    high = x.astype(BF16).astype(F32)
    middle = (x - high).astype(BF16).astype(F32)
    low = (x - high - middle).astype(BF16).astype(F32)
    return high, middle, low


def extend(wide, first, second):
    last = wide[48:56]
    for at, value in enumerate(first + second):
        last = jnp.where(row_of(at + 2, last.shape), value, last)
    return jnp.concatenate([wide[:48], last, jnp.zeros_like(last)], axis=0)


def widen(block_ref, wide_ref):
    depth, blocks, _ = block_ref.shape

    def turn(p, carry):
        full = block_ref[p].astype(F32)
        for half in range(2):
            wide_ref[half, pl.ds(p * blocks, blocks)] = full[:, half * 128 : half * 128 + 128]
        return carry

    lax.fori_loop(0, depth, turn, 0, unroll=5)
    rest = (56 - depth) * blocks
    for half in range(2):
        wide_ref[half, pl.ds(depth * blocks, rest)] = jnp.zeros((rest, 128), F32)


def cluster(wide_ref, blocks, slot):
    halves = [wide_ref[half, pl.ds(slot, 56, stride=blocks)] for half in range(2)]
    return jnp.concatenate(halves, axis=1)


def prepare_target(wide, slot, base, out_ref, top):
    square = jnp.sum(wide * wide, axis=0, keepdims=True)
    out_ref[base + slot] = extend(wide, pieces(-square), (1.0, 1.0, 1.0)).astype(BF16)
    return jnp.maximum(top, square)


def prepare_source(wide, slot, out_ref, top):
    square = jnp.sum(wide * wide, axis=0, keepdims=True)
    full = extend(2.0 * wide, (1.0, 1.0, 1.0), pieces(SHIFT - square))
    out_ref[slot] = full.T.astype(BF16)
    return jnp.maximum(top, square)


def entry(lists_ref, at):
    code = lists_ref[at]
    return lax.shift_right_logical(code, 7), code & 127


def base_of(lists_ref, region):
    base = 0
    for r in range(region):
        base = base + lists_ref[COUNTS + r]
    return base


def in_groups(count, pair):
    def turn(start, ways):
        def body(step, carry):
            for way in range(ways):
                pair(start + step * ways + way)
            return carry

        return body

    groups = count // MANY
    lax.fori_loop(0, groups, turn(0, MANY), 0)
    rest = count - groups * MANY
    lax.fori_loop(0, rest // WAYS, turn(groups * MANY, WAYS), 0)


def first_sweep(region, lists_ref, at_ref, b_ref, k_ref, rows_ref, cols_ref):
    base = base_of(lists_ref, region)

    def pair(at):
        s, w = entry(lists_ref, region * REGION + at)
        logit = jnp.dot(at_ref[s], b_ref[w], preferred_element_type=F32)
        weight = jnp.exp(logit)
        k_ref[base + at] = weight.astype(BF16)
        rows_ref[s] += weight[:, :128] + weight[:, 128:]
        cols_ref[pl.ds(w, 1)] += jnp.sum(weight, axis=0, keepdims=True)

    in_groups(lists_ref[COUNTS + region], pair)


def prepare_kernel(
    source_in, target_in, partners_in, home_in,
    at_ref, b_ref, lists_ref, top_ref,
    source_ref, target_ref, partners_ref, home_ref, sems, source_wide, target_wide,
):
    loads = [
        pltpu.make_async_copy(given, held, sems.at[i])
        for i, (given, held) in enumerate((
            (partners_in, partners_ref), (home_in, home_ref),
            (source_in, source_ref), (target_in, target_ref),
        ))
    ]
    for load in loads:
        load.start()
    for load in loads:
        load.wait()
    links, blocks = partners_ref.shape
    clusters = home_ref.shape[0]
    here = lax.axis_index("cells")
    sibling = 2 - 2 * lax.rem(here, 2)
    cells = source_ref.shape[2]
    widen(source_ref, source_wide)
    widen(target_ref, target_wide)

    regions = jnp.where(sibling == 0, 0b100001, 0b010010)

    def turn(s, carry):
        counts, top = carry
        for m in range(links):
            name = partners_ref[m, s]
            slot = home_ref[jnp.maximum(name, 0)]
            w = slot - (here - 1) * blocks
            w = jnp.where(w < 0, w + clusters, w)
            w = jnp.where(w >= clusters, w - clusters, w)
            block = jnp.where(w >= blocks, 2, 0) + jnp.where(w >= 2 * blocks, 2, 0)
            region = lax.shift_right_logical(regions, block) & 3
            bit = region * 10
            count = lax.shift_right_logical(counts, bit) & 1023
            lists_ref[region * REGION + count] = s * 128 + w
            counts = counts + jnp.where(name >= 0, lax.shift_left(1, bit), 0)
        top = prepare_source(cluster(source_wide, blocks, s), s, at_ref, top)
        top = prepare_target(cluster(target_wide, blocks, s), s, blocks, b_ref, top)
        return counts, top

    counts, top = lax.fori_loop(
        0, blocks, turn, (jnp.int32(0), jnp.zeros((1, cells), F32)), unroll=4
    )
    dummy = 3 * blocks
    for r in range(3):
        count = lax.shift_right_logical(counts, 10 * r) & 1023
        for extra in range(WAYS - 1):
            lists_ref[r * REGION + count + extra] = dummy
        lists_ref[COUNTS + r] = (count + WAYS - 1) // WAYS * WAYS
    shape = b_ref.shape[1:]
    b_ref[dummy] = jnp.where(row_of(50, shape), NEVER, 0.0).astype(BF16)
    top_ref[...] = jnp.broadcast_to(top, top_ref.shape)


def take_block(which, block_ref, b_ref, top_ref, wide_ref):
    blocks = block_ref.shape[1]
    widen(block_ref, wide_ref)
    here = lax.axis_index("cells")
    side = 2 - 2 * lax.rem(here, 2)
    base = (side if which == 1 else 2 - side) * blocks

    def turn(t, top):
        return prepare_target(cluster(wide_ref, blocks, t), t, base, b_ref, top)

    top = lax.fori_loop(0, blocks, turn, top_ref[0:1], unroll=4)
    top_ref[...] = jnp.broadcast_to(top, top_ref.shape)


def within(top_ref):
    return jnp.max(top_ref[0:1]) <= SQ_LIMIT


def near_kernel(
    block_ref, at_ref, lists_ref, b_in, top_in,
    b_ref, top_ref, k_ref, rows_ref, cols_ref, stage_ref, sem, wide_ref,
):
    load = pltpu.make_async_copy(block_ref, stage_ref, sem)
    load.start()
    cols_ref[...] = jnp.zeros(cols_ref.shape, F32)

    def start(s, carry):
        rows_ref[s] = jnp.zeros(rows_ref.shape[1:], F32)
        return carry

    lax.fori_loop(0, rows_ref.shape[0], start, 0, unroll=4)
    load.wait()
    take_block(1, stage_ref, b_ref, top_ref, wide_ref)
    first_sweep(0, lists_ref, at_ref, b_ref, k_ref, rows_ref, cols_ref)
    first_sweep(1, lists_ref, at_ref, b_ref, k_ref, rows_ref, cols_ref)


def each_pair(lists_ref, body):
    for region in range(3):

        def turn(at, carry, region=region):
            body(*entry(lists_ref, region * REGION + at))
            return carry

        lax.fori_loop(0, lists_ref[COUNTS + region], turn, 0)


def careful_rows(lists_ref, at_ref, b_ref, rows_ref, weight_row, out_ref, log_n):
    shape = rows_ref.shape[1:]
    left = lax.broadcasted_iota(jnp.int32, shape, 1) < 64

    def start(s, carry):
        rows_ref[s] = jnp.where(left, NEVER, 0.0)
        return carry

    lax.fori_loop(0, rows_ref.shape[0], start, 0)

    def body(s, w):
        logit = jnp.dot(at_ref[s], b_ref[w], preferred_element_type=F32) + weight_row(w)
        held = rows_ref[s]
        top, total = held[:, 0:1], held[:, 64:65]
        new_top = jnp.maximum(top, jnp.max(logit, axis=1, keepdims=True))
        total = total * jnp.exp(top - new_top)
        total = total + jnp.sum(jnp.exp(logit - new_top), axis=1, keepdims=True)
        rows_ref[s] = jnp.where(left, new_top, total)

    each_pair(lists_ref, body)

    def finish(s, carry):
        held = rows_ref[s]
        lse = held[:, 0:1] + jnp.log(held[:, 64:65]) - SHIFT
        wide = jnp.broadcast_to(lse, shape)
        out_ref[pl.ds(s, 1)] = wide.T[0:1]
        rows_ref[s] = 0.5 * (log_n - wide)
        return carry

    lax.fori_loop(0, rows_ref.shape[0], finish, 0)


def careful_cols(lists_ref, at_ref, b_ref, weight_col, total_ref, out_ref):
    out_ref[...] = jnp.full(out_ref.shape, NEVER, F32)
    total_ref[...] = jnp.zeros(total_ref.shape, F32)

    def body(s, w):
        logit = jnp.dot(at_ref[s], b_ref[w], preferred_element_type=F32)
        logit = logit - SHIFT + weight_col(s)
        at = pl.ds(w, 1)
        top = out_ref[at]
        new_top = jnp.maximum(top, jnp.max(logit, axis=0, keepdims=True))
        total = total_ref[at] * jnp.exp(top - new_top)
        total_ref[at] = total + jnp.sum(jnp.exp(logit - new_top), axis=0, keepdims=True)
        out_ref[at] = new_top

    each_pair(lists_ref, body)
    total = total_ref[...]
    out_ref[...] = jnp.where(
        total > 0.0, out_ref[...] + jnp.log(jnp.maximum(total, 1e-37)), NEVER
    )


def far_kernel(
    log_n,
    block_ref, at_ref, lists_ref, b_in, top_in, k_in, rows_in, cols_in,
    b_ref, top_ref, k_ref, rows_ref, cols_ref, u_ref, row_lse_ref, col_lse_ref, wide_ref,
):
    take_block(2, block_ref, b_ref, top_ref, wide_ref)
    first_sweep(2, lists_ref, at_ref, b_ref, k_ref, rows_ref, cols_ref)
    fine = within(top_ref)

    @pl.when(fine)
    def _():
        total = cols_ref[...]
        col_lse_ref[...] = jnp.where(
            total > 0.0, jnp.log(jnp.maximum(total, 1e-37)) - SHIFT, NEVER
        )
        ones = jnp.ones((128, 128), BF16)

        def turn(s, sums):
            wide = jnp.dot(rows_ref[s].astype(BF16), ones, preferred_element_type=F32)
            u_ref[s] = lax.rsqrt(wide).astype(BF16)
            return jnp.where(lane == s, wide, sums)

        blocks, cells, lanes = rows_ref.shape
        lane = lax.broadcasted_iota(jnp.int32, (cells, lanes), 1)
        sums = lax.fori_loop(0, blocks, turn, jnp.ones((cells, lanes), F32), unroll=4)
        row_lse_ref[...] = jnp.log(sums.T[:blocks]) - SHIFT

    @pl.when(jnp.logical_not(fine))
    def _():
        careful_rows(lists_ref, at_ref, b_ref, rows_ref, lambda w: 0.0, row_lse_ref, log_n)
        careful_cols(lists_ref, at_ref, b_ref, lambda s: 0.0, cols_ref, col_lse_ref)


def column_kernel(
    log_n,
    at_ref, lists_ref, b_ref, top_ref, k_ref, rows_ref, u_ref,
    col_lse_ref, cols_ref,
):
    fine = within(top_ref)

    @pl.when(fine)
    def _():
        cols_ref[...] = jnp.zeros(cols_ref.shape, F32)
        for region in range(3):
            base = base_of(lists_ref, region)

            def pair(at, region=region, base=base):
                s, w = entry(lists_ref, region * REGION + at)
                half = u_ref[s]
                part = k_ref[base + at] * jnp.concatenate([half, half], axis=1)
                while part.shape[0] > 16:
                    mid = part.shape[0] // 2
                    part = part[:mid] + part[mid:]
                cols_ref[pl.ds(w, 1)] += jnp.sum(part.astype(F32), axis=0, keepdims=True)

            in_groups(lists_ref[COUNTS + region], pair)
        total = cols_ref[...]
        col_lse_ref[...] = jnp.where(
            total > 0.0,
            jnp.log(jnp.maximum(total, 1e-37)) + (0.5 * log_n - 0.5 * SHIFT),
            NEVER,
        )

    @pl.when(jnp.logical_not(fine))
    def _():
        careful_cols(
            lists_ref, at_ref, b_ref, lambda s: rows_ref[s][:, 0:1], cols_ref, col_lse_ref
        )


def lse_of(values):
    top = functools.reduce(jnp.maximum, values)
    return top + jnp.log(sum(jnp.exp(v - top) for v in values))


def exchange_kernel(
    log_n, first_ref, second_ref, g_ref, total_ref,
    to_left, to_right, from_left, from_right, from_left2, from_right2, send_sems, receive_sems,
):
    blocks = total_ref.shape[0]
    devices = lax.axis_size("cells")
    here = lax.axis_index("cells")
    peers = [lax.rem(here + devices + step, devices) for step in (-1, 1, -2, 2)]
    barrier = pltpu.get_barrier_semaphore()
    for peer in peers:
        pl.semaphore_signal(
            barrier, inc=1, device_id=(peer,), device_id_type=pl.DeviceIdType.MESH
        )
    to_left[pl.ds(0, 2 * blocks)] = first_ref[pl.ds(0, 2 * blocks)]
    to_left[pl.ds(2 * blocks, blocks)] = second_ref[pl.ds(0, blocks)]
    to_right[pl.ds(0, 2 * blocks)] = first_ref[pl.ds(blocks, 2 * blocks)]
    to_right[pl.ds(2 * blocks, blocks)] = second_ref[pl.ds(2 * blocks, blocks)]
    pl.semaphore_wait(barrier, len(peers))
    copies = []
    for i, (given, taken) in enumerate((
        (to_left, from_right),
        (to_right, from_left),
        (to_left.at[pl.ds(0, blocks)], from_right2),
        (to_right.at[pl.ds(blocks, blocks)], from_left2),
    )):
        copy = pltpu.make_async_remote_copy(
            src_ref=given,
            dst_ref=taken,
            send_sem=send_sems.at[i],
            recv_sem=receive_sems.at[i],
            device_id=(peers[i],),
            device_id_type=pl.DeviceIdType.MESH,
        )
        copy.start()
        copies.append(copy)
    for copy in copies:
        copy.wait()
    low, own, high = (pl.ds(i * blocks, blocks) for i in range(3))
    total_ref[...] = lse_of([second_ref[own], from_right[high], from_left[high]])
    g_ref[...] = jnp.zeros(g_ref.shape, F32)
    for place, values in (
        (low, [first_ref[low], from_left[low], from_left2[...]]),
        (own, [first_ref[own], from_right[low], from_left[own]]),
        (high, [first_ref[high], from_right[own], from_right2[...]]),
    ):
        g_ref[place] = 0.5 * (log_n - lse_of(values))


def row_kernel(
    log_n,
    at_ref, lists_ref, b_ref, top_ref, k_ref, row_lse_ref, g_ref, total_ref, rows_in,
    source_ref, target_ref, rows_ref, second_ref, sums_ref, v_ref,
):
    blocks = source_ref.shape[0]
    target_ref[...] = (0.5 * entropy) * (g_ref[pl.ds(blocks, blocks)] + log_n - total_ref[...])
    g = g_ref[...]
    fine = within(top_ref) & (jnp.max(g) <= 60.0) & (jnp.min(g) >= 0.0)

    @pl.when(fine)
    def _():
        g_line = jnp.exp(g_ref[...] - G_SHIFT)
        for w in range(g_line.shape[0]):
            v_ref[w] = jnp.broadcast_to(g_line[w : w + 1], v_ref.shape[1:]).astype(BF16)

        def start(s, carry):
            sums_ref[s] = jnp.zeros(sums_ref.shape[1:], BF16)
            return carry

        lax.fori_loop(0, blocks, start, 0, unroll=4)
        for region in range(3):
            base = base_of(lists_ref, region)

            def pair(at, region=region, base=base):
                s, w = entry(lists_ref, region * REGION + at)
                line = v_ref[w]
                held = k_ref[base + at]
                part = held.reshape(-1, *line.shape) * line[None]
                part = part.reshape(held.shape)
                sums_ref[s] += part[:, :128] + part[:, 128:]

            in_groups(lists_ref[COUNTS + region], pair)
        wide = (8 * 128, 128)
        group = lax.shift_right_logical(lax.broadcasted_iota(jnp.int32, wide, 0), 7)
        lane = lax.broadcasted_iota(jnp.int32, wide, 1)
        sums = None
        for first in range(0, blocks, 8):
            parts = jnp.concatenate([sums_ref[first + i] for i in range(8)], axis=1)
            pick = jnp.where(lane == group + first, 1.0, 0.0).astype(BF16)
            part = jnp.dot(parts, pick, preferred_element_type=F32)
            sums = part if sums is None else sums + part
        second_ref[...] = jnp.log(sums.T[:blocks]) - SHIFT + G_SHIFT

    @pl.when(jnp.logical_not(fine))
    def _():
        careful_rows(
            lists_ref, at_ref, b_ref, rows_ref, lambda w: g_ref[pl.ds(w, 1)], second_ref, log_n
        )

    first = 0.5 * (log_n - row_lse_ref[...])
    source_ref[...] = (0.5 * entropy) * (first + log_n - second_ref[...])


def in_hbm(array):
    return pltpu.with_memory_space_constraint(array, pltpu.HBM)


def on_device(source_cells, target_cells, partners, home):
    blocks, _, cells = source_cells.shape
    source_cells = source_cells.transpose(1, 0, 2)
    target_cells = target_cells.transpose(1, 0, 2)
    stage = pltpu.VMEM(source_cells.shape, BF16)
    wide = pltpu.VMEM((2, 56 * blocks, 128), F32)
    links = partners.shape[1]
    devices = lax.axis_size("cells")
    log_n = math.log(blocks * devices * cells)
    window = 128
    places = blocks * links + 3 * (WAYS - 1)

    def moved(block, step):
        return lax.ppermute(block, "cells", [(i, step(i) % devices) for i in range(devices)])

    far = moved(target_cells, lambda i: i + 1 if i % 2 else i - 1)
    sibling = in_hbm(moved(target_cells, lambda i: i ^ 1))

    vm = lambda shape, dtype: pltpu.VMEM(shape, dtype)
    at_s = vm((blocks, cells, DEPTH), BF16)
    b_s = vm((3 * blocks + 1, DEPTH, cells), BF16)
    top_s = vm((8, cells), F32)
    k_s = vm((places, cells, cells), BF16)
    rows_s = vm((blocks, cells, 128), F32)
    cols_s = vm((window, cells), F32)
    u_s = vm((blocks, cells, 128), BF16)
    lines_s = vm((blocks, cells), F32)
    limit = pltpu.CompilerParams(vmem_limit_bytes=8 * 2**20)

    at, b, lists, top = pl.pallas_call(
        prepare_kernel,
        out_shape=[at_s, b_s, pltpu.SMEM((COUNTS + 16,), jnp.int32), top_s],
        in_specs=[HBM] * 4,
        out_specs=[VMEM, VMEM, SMEM, VMEM],
        scratch_shapes=[
            stage, stage, pltpu.SMEM((links, blocks), jnp.int32), pltpu.SMEM(home.shape, jnp.int32),
            pltpu.SemaphoreType.DMA((4,)), wide, wide,
        ],
        compiler_params=limit,
        name="prepare",
    )(*map(in_hbm, (source_cells, target_cells, partners.T, home)))
    b, top, k, rows, cols = pl.pallas_call(
        near_kernel,
        out_shape=[b_s, top_s, k_s, rows_s, cols_s],
        in_specs=[HBM, VMEM, SMEM, VMEM, VMEM],
        out_specs=[VMEM] * 5,
        input_output_aliases={3: 0, 4: 1},
        scratch_shapes=[stage, pltpu.SemaphoreType.DMA, wide],
        compiler_params=limit,
        name="near_pairs",
    )(sibling, at, lists, b, top)
    b, top, k, rows, cols, u, row_lse, col_lse = pl.pallas_call(
        functools.partial(far_kernel, log_n),
        out_shape=[b_s, top_s, k_s, rows_s, cols_s, u_s, lines_s, cols_s],
        in_specs=[VMEM, VMEM, SMEM] + [VMEM] * 5,
        out_specs=[VMEM] * 8,
        input_output_aliases={3: 0, 4: 1, 5: 2, 6: 3, 7: 4},
        scratch_shapes=[wide],
        compiler_params=limit,
        name="far_pairs",
    )(far, at, lists, b, top, k, rows, cols)

    col_lse2, _ = pl.pallas_call(
        functools.partial(column_kernel, log_n),
        out_shape=[cols_s, cols_s],
        in_specs=[VMEM, SMEM] + [VMEM] * 5,
        out_specs=[VMEM] * 2,
        compiler_params=limit,
        name="second_columns",
    )(at, lists, b, top, k, rows, u)
    message = pltpu.VMEM((3 * blocks, cells), F32)
    block = pltpu.VMEM((blocks, cells), F32)
    g, total = pl.pallas_call(
        functools.partial(exchange_kernel, log_n),
        out_shape=[cols_s, lines_s],
        in_specs=[VMEM] * 2,
        out_specs=[VMEM] * 2,
        scratch_shapes=[message] * 4 + [block] * 2 + [pltpu.SemaphoreType.DMA((4,))] * 2,
        compiler_params=pltpu.CompilerParams(
            vmem_limit_bytes=8 * 2**20, collective_id=0, has_side_effects=True
        ),
        name="exchange",
    )(col_lse, col_lse2)
    source_pot, target_pot, *_ = pl.pallas_call(
        functools.partial(row_kernel, log_n),
        out_shape=[lines_s, lines_s, rows_s, lines_s, u_s],
        in_specs=[VMEM, SMEM] + [VMEM] * 7,
        out_specs=[VMEM] * 5,
        input_output_aliases={8: 2},
        scratch_shapes=[pltpu.VMEM((window, 16, cells), BF16)],
        compiler_params=limit,
        name="second_rows",
    )(at, lists, b, top, k, row_lse, g, total, rows)
    return source_pot, target_pot


def solution(mesh):
    in_specs = (P("cells", None, None), P("cells", None, None), P("cells", None), P())
    out_specs = (P("cells", None), P("cells", None))
    return jax.shard_map(
        on_device, mesh=mesh, in_specs=in_specs, out_specs=out_specs, check_vma=False
    )
```

```python
import functools
import math

import jax
import jax.numpy as jnp
from jax import lax
from jax.experimental import pallas as pl
from jax.experimental.pallas import tpu as pltpu
from jax.sharding import PartitionSpec as P

F32 = jnp.float32
BF16 = jnp.bfloat16
entropy = 0.5
SHIFT = 48.0
SQ_LIMIT = 24.0
G_SHIFT = 24.0
NEVER = -1e30
WAYS = 2
MANY = 16
DEPTH = 64
REGION = 256
COUNTS = 3 * REGION

VMEM = pl.BlockSpec(memory_space=pltpu.VMEM)
HBM = pl.BlockSpec(memory_space=pltpu.HBM)
SMEM = pl.BlockSpec(memory_space=pltpu.SMEM)


def row_of(index, shape):
    return lax.broadcasted_iota(jnp.int32, shape, 0) == index


def pieces(x):
    high = x.astype(BF16).astype(F32)
    middle = (x - high).astype(BF16).astype(F32)
    low = (x - high - middle).astype(BF16).astype(F32)
    return high, middle, low


def extend(wide, first, second):
    last = wide[48:56]
    for at, value in enumerate(first + second):
        last = jnp.where(row_of(at + 2, last.shape), value, last)
    return jnp.concatenate([wide[:48], last, jnp.zeros_like(last)], axis=0)


def widen(block_ref, wide_ref):
    depth, blocks, _ = block_ref.shape

    def turn(p, carry):
        full = block_ref[p].astype(F32)
        for half in range(2):
            wide_ref[half, pl.ds(p * blocks, blocks)] = full[:, half * 128 : half * 128 + 128]
        return carry

    lax.fori_loop(0, depth, turn, 0, unroll=10)
    rest = (56 - depth) * blocks
    for half in range(2):
        wide_ref[half, pl.ds(depth * blocks, rest)] = jnp.zeros((rest, 128), F32)


def cluster(wide_ref, blocks, slot):
    halves = [wide_ref[half, pl.ds(slot, 56, stride=blocks)] for half in range(2)]
    return jnp.concatenate(halves, axis=1)


def prepare_target(wide, slot, base, out_ref, top):
    square = jnp.sum(wide * wide, axis=0, keepdims=True)
    out_ref[base + slot] = extend(wide, pieces(-square), (1.0, 1.0, 1.0)).astype(BF16)
    return jnp.maximum(top, square)


def prepare_source(wide, slot, out_ref, top):
    square = jnp.sum(wide * wide, axis=0, keepdims=True)
    full = extend(2.0 * wide, (1.0, 1.0, 1.0), pieces(SHIFT - square))
    out_ref[slot] = full.T.astype(BF16)
    return jnp.maximum(top, square)


def entry(lists_ref, at):
    code = lists_ref[at]
    return lax.shift_right_logical(code, 7), code & 127


def base_of(lists_ref, region):
    base = 0
    for r in range(region):
        base = base + lists_ref[COUNTS + r]
    return base


def in_groups(count, pair):
    def turn(start, ways):
        def body(step, carry):
            for way in range(ways):
                pair(start + step * ways + way)
            return carry

        return body

    groups = count // MANY
    lax.fori_loop(0, groups, turn(0, MANY), 0)
    rest = count - groups * MANY
    lax.fori_loop(0, rest // WAYS, turn(groups * MANY, WAYS), 0)


def first_sweep(region, lists_ref, at_ref, b_ref, k_ref, rows_ref, cols_ref):
    base = base_of(lists_ref, region)

    def pair(at):
        s, w = entry(lists_ref, region * REGION + at)
        logit = jnp.dot(at_ref[s], b_ref[w], preferred_element_type=F32)
        weight = jnp.exp(logit)
        k_ref[base + at] = weight.astype(BF16)
        rows_ref[s] += weight[:, :128] + weight[:, 128:]
        cols_ref[pl.ds(w, 1)] += jnp.sum(weight, axis=0, keepdims=True)

    in_groups(lists_ref[COUNTS + region], pair)


def prepare_kernel(
    source_in, target_in, partners_in, home_in,
    at_ref, b_ref, lists_ref, top_ref,
    source_ref, target_ref, partners_ref, home_ref, sems, source_wide, target_wide,
):
    loads = [
        pltpu.make_async_copy(given, held, sems.at[i])
        for i, (given, held) in enumerate((
            (partners_in, partners_ref), (home_in, home_ref),
            (source_in, source_ref), (target_in, target_ref),
        ))
    ]
    for load in loads:
        load.start()
    for load in loads:
        load.wait()
    links, blocks = partners_ref.shape
    clusters = home_ref.shape[0]
    here = lax.axis_index("cells")
    sibling = 2 - 2 * lax.rem(here, 2)
    cells = source_ref.shape[2]
    widen(source_ref, source_wide)
    widen(target_ref, target_wide)

    regions = jnp.where(sibling == 0, 0b100001, 0b010010)

    def turn(s, carry):
        counts, top = carry
        for m in range(links):
            name = partners_ref[m, s]
            slot = home_ref[jnp.maximum(name, 0)]
            w = slot - (here - 1) * blocks
            w = jnp.where(w < 0, w + clusters, w)
            w = jnp.where(w >= clusters, w - clusters, w)
            block = jnp.where(w >= blocks, 2, 0) + jnp.where(w >= 2 * blocks, 2, 0)
            region = lax.shift_right_logical(regions, block) & 3
            bit = region * 10
            count = lax.shift_right_logical(counts, bit) & 1023
            lists_ref[region * REGION + count] = s * 128 + w
            counts = counts + jnp.where(name >= 0, lax.shift_left(1, bit), 0)
        top = prepare_source(cluster(source_wide, blocks, s), s, at_ref, top)
        top = prepare_target(cluster(target_wide, blocks, s), s, blocks, b_ref, top)
        return counts, top

    counts, top = lax.fori_loop(
        0, blocks, turn, (jnp.int32(0), jnp.zeros((1, cells), F32)), unroll=4
    )
    dummy = 3 * blocks
    for r in range(3):
        count = lax.shift_right_logical(counts, 10 * r) & 1023
        for extra in range(WAYS - 1):
            lists_ref[r * REGION + count + extra] = dummy
        lists_ref[COUNTS + r] = (count + WAYS - 1) // WAYS * WAYS
    shape = b_ref.shape[1:]
    b_ref[dummy] = jnp.where(row_of(50, shape), NEVER, 0.0).astype(BF16)
    top_ref[...] = jnp.broadcast_to(top, top_ref.shape)


def take_block(which, block_ref, b_ref, top_ref, wide_ref):
    blocks = block_ref.shape[1]
    widen(block_ref, wide_ref)
    here = lax.axis_index("cells")
    side = 2 - 2 * lax.rem(here, 2)
    base = (side if which == 1 else 2 - side) * blocks

    def turn(t, top):
        return prepare_target(cluster(wide_ref, blocks, t), t, base, b_ref, top)

    top = lax.fori_loop(0, blocks, turn, top_ref[0:1], unroll=8)
    top_ref[...] = jnp.broadcast_to(top, top_ref.shape)


def within(top_ref):
    return jnp.max(top_ref[0:1]) <= SQ_LIMIT


def near_kernel(
    block_ref, at_ref, lists_ref, b_in, top_in,
    b_ref, top_ref, k_ref, rows_ref, cols_ref, stage_ref, sem, wide_ref,
):
    load = pltpu.make_async_copy(block_ref, stage_ref, sem)
    load.start()
    cols_ref[...] = jnp.zeros(cols_ref.shape, F32)

    def start(s, carry):
        rows_ref[s] = jnp.zeros(rows_ref.shape[1:], F32)
        return carry

    lax.fori_loop(0, rows_ref.shape[0], start, 0, unroll=4)
    load.wait()
    take_block(1, stage_ref, b_ref, top_ref, wide_ref)
    first_sweep(0, lists_ref, at_ref, b_ref, k_ref, rows_ref, cols_ref)
    first_sweep(1, lists_ref, at_ref, b_ref, k_ref, rows_ref, cols_ref)


def each_pair(lists_ref, body):
    for region in range(3):

        def turn(at, carry, region=region):
            body(*entry(lists_ref, region * REGION + at))
            return carry

        lax.fori_loop(0, lists_ref[COUNTS + region], turn, 0)


def careful_rows(lists_ref, at_ref, b_ref, rows_ref, weight_row, out_ref, log_n):
    shape = rows_ref.shape[1:]
    left = lax.broadcasted_iota(jnp.int32, shape, 1) < 64

    def start(s, carry):
        rows_ref[s] = jnp.where(left, NEVER, 0.0)
        return carry

    lax.fori_loop(0, rows_ref.shape[0], start, 0)

    def body(s, w):
        logit = jnp.dot(at_ref[s], b_ref[w], preferred_element_type=F32) + weight_row(w)
        held = rows_ref[s]
        top, total = held[:, 0:1], held[:, 64:65]
        new_top = jnp.maximum(top, jnp.max(logit, axis=1, keepdims=True))
        total = total * jnp.exp(top - new_top)
        total = total + jnp.sum(jnp.exp(logit - new_top), axis=1, keepdims=True)
        rows_ref[s] = jnp.where(left, new_top, total)

    each_pair(lists_ref, body)

    def finish(s, carry):
        held = rows_ref[s]
        lse = held[:, 0:1] + jnp.log(held[:, 64:65]) - SHIFT
        wide = jnp.broadcast_to(lse, shape)
        out_ref[pl.ds(s, 1)] = wide.T[0:1]
        rows_ref[s] = 0.5 * (log_n - wide)
        return carry

    lax.fori_loop(0, rows_ref.shape[0], finish, 0)


def careful_cols(lists_ref, at_ref, b_ref, weight_col, total_ref, out_ref):
    out_ref[...] = jnp.full(out_ref.shape, NEVER, F32)
    total_ref[...] = jnp.zeros(total_ref.shape, F32)

    def body(s, w):
        logit = jnp.dot(at_ref[s], b_ref[w], preferred_element_type=F32)
        logit = logit - SHIFT + weight_col(s)
        at = pl.ds(w, 1)
        top = out_ref[at]
        new_top = jnp.maximum(top, jnp.max(logit, axis=0, keepdims=True))
        total = total_ref[at] * jnp.exp(top - new_top)
        total_ref[at] = total + jnp.sum(jnp.exp(logit - new_top), axis=0, keepdims=True)
        out_ref[at] = new_top

    each_pair(lists_ref, body)
    total = total_ref[...]
    out_ref[...] = jnp.where(
        total > 0.0, out_ref[...] + jnp.log(jnp.maximum(total, 1e-37)), NEVER
    )


def far_kernel(
    log_n,
    block_ref, at_ref, lists_ref, b_in, top_in, k_in, rows_in, cols_in,
    b_ref, top_ref, k_ref, rows_ref, cols_ref, u_ref, row_lse_ref, col_lse_ref, wide_ref,
):
    take_block(2, block_ref, b_ref, top_ref, wide_ref)
    first_sweep(2, lists_ref, at_ref, b_ref, k_ref, rows_ref, cols_ref)
    fine = within(top_ref)

    @pl.when(fine)
    def _():
        total = cols_ref[...]
        col_lse_ref[...] = jnp.where(
            total > 0.0, jnp.log(jnp.maximum(total, 1e-37)) - SHIFT, NEVER
        )
        ones = jnp.ones((128, 128), BF16)

        def turn(s, sums):
            wide = jnp.dot(rows_ref[s].astype(BF16), ones, preferred_element_type=F32)
            u_ref[s] = lax.rsqrt(wide).astype(BF16)
            return jnp.where(lane == s, wide, sums)

        blocks, cells, lanes = rows_ref.shape
        lane = lax.broadcasted_iota(jnp.int32, (cells, lanes), 1)
        sums = lax.fori_loop(0, blocks, turn, jnp.ones((cells, lanes), F32), unroll=20)
        row_lse_ref[...] = jnp.log(sums.T[:blocks]) - SHIFT

    @pl.when(jnp.logical_not(fine))
    def _():
        careful_rows(lists_ref, at_ref, b_ref, rows_ref, lambda w: 0.0, row_lse_ref, log_n)
        careful_cols(lists_ref, at_ref, b_ref, lambda s: 0.0, cols_ref, col_lse_ref)


def column_kernel(
    log_n,
    at_ref, lists_ref, b_ref, top_ref, k_ref, rows_ref, u_ref,
    col_lse_ref, cols_ref,
):
    fine = within(top_ref)

    @pl.when(fine)
    def _():
        cols_ref[...] = jnp.zeros(cols_ref.shape, F32)
        for region in range(3):
            base = base_of(lists_ref, region)

            def pair(at, region=region, base=base):
                s, w = entry(lists_ref, region * REGION + at)
                half = u_ref[s]
                part = k_ref[base + at] * jnp.concatenate([half, half], axis=1)
                while part.shape[0] > 16:
                    mid = part.shape[0] // 2
                    part = part[:mid] + part[mid:]
                cols_ref[pl.ds(w, 1)] += jnp.sum(part.astype(F32), axis=0, keepdims=True)

            in_groups(lists_ref[COUNTS + region], pair)
        total = cols_ref[...]
        col_lse_ref[...] = jnp.where(
            total > 0.0,
            jnp.log(jnp.maximum(total, 1e-37)) + (0.5 * log_n - 0.5 * SHIFT),
            NEVER,
        )

    @pl.when(jnp.logical_not(fine))
    def _():
        careful_cols(
            lists_ref, at_ref, b_ref, lambda s: rows_ref[s][:, 0:1], cols_ref, col_lse_ref
        )


def lse_of(values):
    top = functools.reduce(jnp.maximum, values)
    return top + jnp.log(sum(jnp.exp(v - top) for v in values))


def exchange_kernel(
    log_n, first_ref, second_ref, g_ref, total_ref,
    to_left, to_right, from_left, from_right, from_left2, from_right2, send_sems, receive_sems,
):
    blocks = total_ref.shape[0]
    devices = lax.axis_size("cells")
    here = lax.axis_index("cells")
    peers = [lax.rem(here + devices + step, devices) for step in (-1, 1, -2, 2)]
    barrier = pltpu.get_barrier_semaphore()
    for peer in peers:
        pl.semaphore_signal(
            barrier, inc=1, device_id=(peer,), device_id_type=pl.DeviceIdType.MESH
        )
    to_left[pl.ds(0, 2 * blocks)] = first_ref[pl.ds(0, 2 * blocks)]
    to_left[pl.ds(2 * blocks, blocks)] = second_ref[pl.ds(0, blocks)]
    to_right[pl.ds(0, 2 * blocks)] = first_ref[pl.ds(blocks, 2 * blocks)]
    to_right[pl.ds(2 * blocks, blocks)] = second_ref[pl.ds(2 * blocks, blocks)]
    pl.semaphore_wait(barrier, len(peers))
    copies = []
    for i, (given, taken) in enumerate((
        (to_left, from_right),
        (to_right, from_left),
        (to_left.at[pl.ds(0, blocks)], from_right2),
        (to_right.at[pl.ds(blocks, blocks)], from_left2),
    )):
        copy = pltpu.make_async_remote_copy(
            src_ref=given,
            dst_ref=taken,
            send_sem=send_sems.at[i],
            recv_sem=receive_sems.at[i],
            device_id=(peers[i],),
            device_id_type=pl.DeviceIdType.MESH,
        )
        copy.start()
        copies.append(copy)
    for copy in copies:
        copy.wait()
    low, own, high = (pl.ds(i * blocks, blocks) for i in range(3))
    total_ref[...] = lse_of([second_ref[own], from_right[high], from_left[high]])
    g_ref[...] = jnp.zeros(g_ref.shape, F32)
    for place, values in (
        (low, [first_ref[low], from_left[low], from_left2[...]]),
        (own, [first_ref[own], from_right[low], from_left[own]]),
        (high, [first_ref[high], from_right[own], from_right2[...]]),
    ):
        g_ref[place] = 0.5 * (log_n - lse_of(values))


def row_kernel(
    log_n,
    at_ref, lists_ref, b_ref, top_ref, k_ref, row_lse_ref, g_ref, total_ref, rows_in,
    source_ref, target_ref, rows_ref, second_ref, sums_ref, v_ref,
):
    blocks = source_ref.shape[0]
    target_ref[...] = (0.5 * entropy) * (g_ref[pl.ds(blocks, blocks)] + log_n - total_ref[...])
    g = g_ref[...]
    fine = within(top_ref) & (jnp.max(g) <= 60.0) & (jnp.min(g) >= 0.0)

    @pl.when(fine)
    def _():
        g_line = jnp.exp(g_ref[...] - G_SHIFT)
        for w in range(g_line.shape[0]):
            v_ref[w] = jnp.broadcast_to(g_line[w : w + 1], v_ref.shape[1:]).astype(BF16)

        def start(s, carry):
            sums_ref[s] = jnp.zeros(sums_ref.shape[1:], BF16)
            return carry

        lax.fori_loop(0, blocks, start, 0, unroll=8)
        for region in range(3):
            base = base_of(lists_ref, region)

            def pair(at, region=region, base=base):
                s, w = entry(lists_ref, region * REGION + at)
                line = v_ref[w]
                held = k_ref[base + at]
                part = held.reshape(-1, *line.shape) * line[None]
                part = part.reshape(held.shape)
                sums_ref[s] += part[:, :128] + part[:, 128:]

            in_groups(lists_ref[COUNTS + region], pair)
        wide = (8 * 128, 128)
        group = lax.shift_right_logical(lax.broadcasted_iota(jnp.int32, wide, 0), 7)
        lane = lax.broadcasted_iota(jnp.int32, wide, 1)
        sums = None
        for first in range(0, blocks, 8):
            parts = jnp.concatenate([sums_ref[first + i] for i in range(8)], axis=1)
            pick = jnp.where(lane == group + first, 1.0, 0.0).astype(BF16)
            part = jnp.dot(parts, pick, preferred_element_type=F32)
            sums = part if sums is None else sums + part
        second_ref[...] = jnp.log(sums.T[:blocks]) - SHIFT + G_SHIFT

    @pl.when(jnp.logical_not(fine))
    def _():
        careful_rows(
            lists_ref, at_ref, b_ref, rows_ref, lambda w: g_ref[pl.ds(w, 1)], second_ref, log_n
        )

    first = 0.5 * (log_n - row_lse_ref[...])
    source_ref[...] = (0.5 * entropy) * (first + log_n - second_ref[...])


def in_hbm(array):
    return pltpu.with_memory_space_constraint(array, pltpu.HBM)


def on_device(source_cells, target_cells, partners, home):
    blocks, _, cells = source_cells.shape
    source_cells = source_cells.transpose(1, 0, 2)
    target_cells = target_cells.transpose(1, 0, 2)
    stage = pltpu.VMEM(source_cells.shape, BF16)
    wide = pltpu.VMEM((2, 56 * blocks, 128), F32)
    links = partners.shape[1]
    devices = lax.axis_size("cells")
    log_n = math.log(blocks * devices * cells)
    window = 128
    places = blocks * links + 3 * (WAYS - 1)

    def moved(block, step):
        return lax.ppermute(block, "cells", [(i, step(i) % devices) for i in range(devices)])

    far = moved(target_cells, lambda i: i + 1 if i % 2 else i - 1)
    sibling = in_hbm(moved(target_cells, lambda i: i ^ 1))

    vm = lambda shape, dtype: pltpu.VMEM(shape, dtype)
    at_s = vm((blocks, cells, DEPTH), BF16)
    b_s = vm((3 * blocks + 1, DEPTH, cells), BF16)
    top_s = vm((8, cells), F32)
    k_s = vm((places, cells, cells), BF16)
    rows_s = vm((blocks, cells, 128), F32)
    cols_s = vm((window, cells), F32)
    u_s = vm((blocks, cells, 128), BF16)
    lines_s = vm((blocks, cells), F32)
    limit = pltpu.CompilerParams(vmem_limit_bytes=8 * 2**20)

    at, b, lists, top = pl.pallas_call(
        prepare_kernel,
        out_shape=[at_s, b_s, pltpu.SMEM((COUNTS + 16,), jnp.int32), top_s],
        in_specs=[HBM] * 4,
        out_specs=[VMEM, VMEM, SMEM, VMEM],
        scratch_shapes=[
            stage, stage, pltpu.SMEM((links, blocks), jnp.int32), pltpu.SMEM(home.shape, jnp.int32),
            pltpu.SemaphoreType.DMA((4,)), wide, wide,
        ],
        compiler_params=limit,
        name="prepare",
    )(*map(in_hbm, (source_cells, target_cells, partners.T, home)))
    b, top, k, rows, cols = pl.pallas_call(
        near_kernel,
        out_shape=[b_s, top_s, k_s, rows_s, cols_s],
        in_specs=[HBM, VMEM, SMEM, VMEM, VMEM],
        out_specs=[VMEM] * 5,
        input_output_aliases={3: 0, 4: 1},
        scratch_shapes=[stage, pltpu.SemaphoreType.DMA, wide],
        compiler_params=limit,
        name="near_pairs",
    )(sibling, at, lists, b, top)
    b, top, k, rows, cols, u, row_lse, col_lse = pl.pallas_call(
        functools.partial(far_kernel, log_n),
        out_shape=[b_s, top_s, k_s, rows_s, cols_s, u_s, lines_s, cols_s],
        in_specs=[VMEM, VMEM, SMEM] + [VMEM] * 5,
        out_specs=[VMEM] * 8,
        input_output_aliases={3: 0, 4: 1, 5: 2, 6: 3, 7: 4},
        scratch_shapes=[wide],
        compiler_params=limit,
        name="far_pairs",
    )(far, at, lists, b, top, k, rows, cols)

    col_lse2, _ = pl.pallas_call(
        functools.partial(column_kernel, log_n),
        out_shape=[cols_s, cols_s],
        in_specs=[VMEM, SMEM] + [VMEM] * 5,
        out_specs=[VMEM] * 2,
        compiler_params=limit,
        name="second_columns",
    )(at, lists, b, top, k, rows, u)
    result = jax.ShapeDtypeStruct((blocks, cells), F32)
    message = pltpu.VMEM((3 * blocks, cells), F32)
    block = pltpu.VMEM((blocks, cells), F32)
    g, total = pl.pallas_call(
        functools.partial(exchange_kernel, log_n),
        out_shape=[cols_s, lines_s],
        in_specs=[VMEM] * 2,
        out_specs=[VMEM] * 2,
        scratch_shapes=[message] * 4 + [block] * 2 + [pltpu.SemaphoreType.DMA((4,))] * 2,
        compiler_params=pltpu.CompilerParams(
            vmem_limit_bytes=8 * 2**20, collective_id=0, has_side_effects=True
        ),
        name="exchange",
    )(col_lse, col_lse2)
    source_pot, target_pot, *_ = pl.pallas_call(
        functools.partial(row_kernel, log_n),
        out_shape=[result, result, rows_s, lines_s, u_s],
        in_specs=[VMEM, SMEM] + [VMEM] * 7,
        out_specs=[VMEM] * 5,
        input_output_aliases={8: 2},
        scratch_shapes=[pltpu.VMEM((window, 16, cells), BF16)],
        compiler_params=limit,
        name="second_rows",
    )(at, lists, b, top, k, row_lse, g, total, rows)
    return source_pot, target_pot


def solution(mesh):
    in_specs = (P("cells", None, None), P("cells", None, None), P("cells", None), P())
    out_specs = (P("cells", None), P("cells", None))
    return jax.shard_map(
        on_device, mesh=mesh, in_specs=in_specs, out_specs=out_specs, check_vma=False
    )
```

```python
import functools
import math

import jax
import jax.numpy as jnp
from jax import lax
from jax.experimental import pallas as pl
from jax.experimental.pallas import tpu as pltpu
from jax.sharding import PartitionSpec as P

F32 = jnp.float32
BF16 = jnp.bfloat16
entropy = 0.5
SHIFT = 48.0
SQ_LIMIT = 24.0
G_SHIFT = 24.0
NEVER = -1e30
WAYS = 2
MANY = 16
SOME = 6
DEPTH = 64
REGION = 256
COUNTS = 3 * REGION

VMEM = pl.BlockSpec(memory_space=pltpu.VMEM)
HBM = pl.BlockSpec(memory_space=pltpu.HBM)
SMEM = pl.BlockSpec(memory_space=pltpu.SMEM)


def row_of(index, shape):
    return lax.broadcasted_iota(jnp.int32, shape, 0) == index


def pieces(x):
    high = x.astype(BF16).astype(F32)
    middle = (x - high).astype(BF16).astype(F32)
    low = (x - high - middle).astype(BF16).astype(F32)
    return high, middle, low


def extend(wide, first, second):
    last = wide[48:56]
    for at, value in enumerate(first + second):
        last = jnp.where(row_of(at + 2, last.shape), value, last)
    return jnp.concatenate([wide[:48], last, jnp.zeros_like(last)], axis=0)


def widen(block_ref, wide_ref):
    depth, blocks, _ = block_ref.shape

    def turn(p, carry):
        full = block_ref[p].astype(F32)
        for half in range(2):
            wide_ref[half, pl.ds(p * blocks, blocks)] = full[:, half * 128 : half * 128 + 128]
        return carry

    lax.fori_loop(0, depth, turn, 0, unroll=10)
    rest = (56 - depth) * blocks
    for half in range(2):
        wide_ref[half, pl.ds(depth * blocks, rest)] = jnp.zeros((rest, 128), F32)


def cluster(wide_ref, blocks, slot):
    halves = [wide_ref[half, pl.ds(slot, 56, stride=blocks)] for half in range(2)]
    return jnp.concatenate(halves, axis=1)


def prepare_target(wide, slot, base, out_ref, top):
    square = jnp.sum(wide * wide, axis=0, keepdims=True)
    out_ref[base + slot] = extend(wide, pieces(-square), (1.0, 1.0, 1.0)).astype(BF16)
    return jnp.maximum(top, square)


def prepare_source(wide, slot, out_ref, top):
    square = jnp.sum(wide * wide, axis=0, keepdims=True)
    full = extend(2.0 * wide, (1.0, 1.0, 1.0), pieces(SHIFT - square))
    out_ref[slot] = full.T.astype(BF16)
    return jnp.maximum(top, square)


def entry(lists_ref, at):
    code = lists_ref[at]
    return lax.shift_right_logical(code, 7), code & 127


def base_of(lists_ref, region):
    base = 0
    for r in range(region):
        base = base + lists_ref[COUNTS + r]
    return base


def in_groups(count, pair):
    def turn(start, ways):
        def body(step, carry):
            for way in range(ways):
                pair(start + step * ways + way)
            return carry

        return body

    done = 0
    for ways in (MANY, SOME, WAYS):
        groups = (count - done) // ways
        lax.fori_loop(0, groups, turn(done, ways), 0)
        done = done + groups * ways


def first_sweep(region, lists_ref, at_ref, b_ref, k_ref, rows_ref, cols_ref):
    base = base_of(lists_ref, region)

    def pair(at):
        s, w = entry(lists_ref, region * REGION + at)
        logit = jnp.dot(at_ref[s], b_ref[w], preferred_element_type=F32)
        weight = jnp.exp(logit)
        k_ref[base + at] = weight.astype(BF16)
        rows_ref[s] += weight[:, :128] + weight[:, 128:]
        cols_ref[pl.ds(w, 1)] += jnp.sum(weight, axis=0, keepdims=True)

    in_groups(lists_ref[COUNTS + region], pair)


def prepare_kernel(
    source_in, target_in, partners_in, home_in,
    at_ref, b_ref, lists_ref, top_ref,
    source_ref, target_ref, partners_ref, home_ref, sems, source_wide, target_wide,
):
    loads = [
        pltpu.make_async_copy(given, held, sems.at[i])
        for i, (given, held) in enumerate((
            (partners_in, partners_ref), (home_in, home_ref),
            (source_in, source_ref), (target_in, target_ref),
        ))
    ]
    for load in loads:
        load.start()
    for load in loads:
        load.wait()
    links, blocks = partners_ref.shape
    clusters = home_ref.shape[0]
    here = lax.axis_index("cells")
    sibling = 2 - 2 * lax.rem(here, 2)
    cells = source_ref.shape[2]
    widen(source_ref, source_wide)
    widen(target_ref, target_wide)

    regions = jnp.where(sibling == 0, 0b100001, 0b010010)

    def turn(s, carry):
        counts, top = carry
        for m in range(links):
            name = partners_ref[m, s]
            slot = home_ref[jnp.maximum(name, 0)]
            w = slot - (here - 1) * blocks
            w = jnp.where(w < 0, w + clusters, w)
            w = jnp.where(w >= clusters, w - clusters, w)
            block = jnp.where(w >= blocks, 2, 0) + jnp.where(w >= 2 * blocks, 2, 0)
            region = lax.shift_right_logical(regions, block) & 3
            bit = region * 10
            count = lax.shift_right_logical(counts, bit) & 1023
            lists_ref[region * REGION + count] = s * 128 + w
            counts = counts + jnp.where(name >= 0, lax.shift_left(1, bit), 0)
        top = prepare_source(cluster(source_wide, blocks, s), s, at_ref, top)
        top = prepare_target(cluster(target_wide, blocks, s), s, blocks, b_ref, top)
        return counts, top

    counts, top = lax.fori_loop(
        0, blocks, turn, (jnp.int32(0), jnp.zeros((1, cells), F32)), unroll=4
    )
    dummy = 3 * blocks
    for r in range(3):
        count = lax.shift_right_logical(counts, 10 * r) & 1023
        for extra in range(WAYS - 1):
            lists_ref[r * REGION + count + extra] = dummy
        lists_ref[COUNTS + r] = (count + WAYS - 1) // WAYS * WAYS
    shape = b_ref.shape[1:]
    b_ref[dummy] = jnp.where(row_of(50, shape), NEVER, 0.0).astype(BF16)
    top_ref[...] = jnp.broadcast_to(top, top_ref.shape)


def take_block(which, block_ref, b_ref, top_ref, wide_ref):
    blocks = block_ref.shape[1]
    widen(block_ref, wide_ref)
    here = lax.axis_index("cells")
    side = 2 - 2 * lax.rem(here, 2)
    base = (side if which == 1 else 2 - side) * blocks

    def turn(t, top):
        return prepare_target(cluster(wide_ref, blocks, t), t, base, b_ref, top)

    top = lax.fori_loop(0, blocks, turn, top_ref[0:1], unroll=8)
    top_ref[...] = jnp.broadcast_to(top, top_ref.shape)


def within(top_ref):
    return jnp.max(top_ref[0:1]) <= SQ_LIMIT


def near_kernel(
    block_ref, at_ref, lists_ref, b_in, top_in,
    b_ref, top_ref, k_ref, rows_ref, cols_ref, stage_ref, sem, wide_ref,
):
    load = pltpu.make_async_copy(block_ref, stage_ref, sem)
    load.start()
    cols_ref[...] = jnp.zeros(cols_ref.shape, F32)

    def start(s, carry):
        rows_ref[s] = jnp.zeros(rows_ref.shape[1:], F32)
        return carry

    lax.fori_loop(0, rows_ref.shape[0], start, 0, unroll=4)
    load.wait()
    take_block(1, stage_ref, b_ref, top_ref, wide_ref)
    first_sweep(0, lists_ref, at_ref, b_ref, k_ref, rows_ref, cols_ref)
    first_sweep(1, lists_ref, at_ref, b_ref, k_ref, rows_ref, cols_ref)


def each_pair(lists_ref, body):
    for region in range(3):

        def turn(at, carry, region=region):
            body(*entry(lists_ref, region * REGION + at))
            return carry

        lax.fori_loop(0, lists_ref[COUNTS + region], turn, 0)


def careful_rows(lists_ref, at_ref, b_ref, rows_ref, weight_row, out_ref, log_n):
    shape = rows_ref.shape[1:]
    left = lax.broadcasted_iota(jnp.int32, shape, 1) < 64

    def start(s, carry):
        rows_ref[s] = jnp.where(left, NEVER, 0.0)
        return carry

    lax.fori_loop(0, rows_ref.shape[0], start, 0)

    def body(s, w):
        logit = jnp.dot(at_ref[s], b_ref[w], preferred_element_type=F32) + weight_row(w)
        held = rows_ref[s]
        top, total = held[:, 0:1], held[:, 64:65]
        new_top = jnp.maximum(top, jnp.max(logit, axis=1, keepdims=True))
        total = total * jnp.exp(top - new_top)
        total = total + jnp.sum(jnp.exp(logit - new_top), axis=1, keepdims=True)
        rows_ref[s] = jnp.where(left, new_top, total)

    each_pair(lists_ref, body)

    def finish(s, carry):
        held = rows_ref[s]
        lse = held[:, 0:1] + jnp.log(held[:, 64:65]) - SHIFT
        wide = jnp.broadcast_to(lse, shape)
        out_ref[pl.ds(s, 1)] = wide.T[0:1]
        rows_ref[s] = 0.5 * (log_n - wide)
        return carry

    lax.fori_loop(0, rows_ref.shape[0], finish, 0)


def careful_cols(lists_ref, at_ref, b_ref, weight_col, total_ref, out_ref):
    out_ref[...] = jnp.full(out_ref.shape, NEVER, F32)
    total_ref[...] = jnp.zeros(total_ref.shape, F32)

    def body(s, w):
        logit = jnp.dot(at_ref[s], b_ref[w], preferred_element_type=F32)
        logit = logit - SHIFT + weight_col(s)
        at = pl.ds(w, 1)
        top = out_ref[at]
        new_top = jnp.maximum(top, jnp.max(logit, axis=0, keepdims=True))
        total = total_ref[at] * jnp.exp(top - new_top)
        total_ref[at] = total + jnp.sum(jnp.exp(logit - new_top), axis=0, keepdims=True)
        out_ref[at] = new_top

    each_pair(lists_ref, body)
    total = total_ref[...]
    out_ref[...] = jnp.where(
        total > 0.0, out_ref[...] + jnp.log(jnp.maximum(total, 1e-37)), NEVER
    )


def far_kernel(
    log_n,
    block_ref, at_ref, lists_ref, b_in, top_in, k_in, rows_in, cols_in,
    b_ref, top_ref, k_ref, rows_ref, cols_ref, u_ref, row_lse_ref, col_lse_ref, wide_ref,
):
    take_block(2, block_ref, b_ref, top_ref, wide_ref)
    first_sweep(2, lists_ref, at_ref, b_ref, k_ref, rows_ref, cols_ref)
    fine = within(top_ref)

    @pl.when(fine)
    def _():
        total = cols_ref[...]
        col_lse_ref[...] = jnp.where(
            total > 0.0, jnp.log(jnp.maximum(total, 1e-37)) - SHIFT, NEVER
        )
        ones = jnp.ones((128, 128), BF16)

        def turn(s, sums):
            wide = jnp.dot(rows_ref[s].astype(BF16), ones, preferred_element_type=F32)
            u_ref[s] = lax.rsqrt(wide).astype(BF16)
            return jnp.where(lane == s, wide, sums)

        blocks, cells, lanes = rows_ref.shape
        lane = lax.broadcasted_iota(jnp.int32, (cells, lanes), 1)
        sums = lax.fori_loop(0, blocks, turn, jnp.ones((cells, lanes), F32), unroll=20)
        row_lse_ref[...] = jnp.log(sums.T[:blocks]) - SHIFT

    @pl.when(jnp.logical_not(fine))
    def _():
        careful_rows(lists_ref, at_ref, b_ref, rows_ref, lambda w: 0.0, row_lse_ref, log_n)
        careful_cols(lists_ref, at_ref, b_ref, lambda s: 0.0, cols_ref, col_lse_ref)


def column_kernel(
    log_n,
    at_ref, lists_ref, b_ref, top_ref, k_ref, rows_ref, u_ref,
    col_lse_ref, cols_ref,
):
    fine = within(top_ref)

    @pl.when(fine)
    def _():
        cols_ref[...] = jnp.zeros(cols_ref.shape, F32)
        for region in range(3):
            base = base_of(lists_ref, region)

            def pair(at, region=region, base=base):
                s, w = entry(lists_ref, region * REGION + at)
                half = u_ref[s]
                part = k_ref[base + at] * jnp.concatenate([half, half], axis=1)
                while part.shape[0] > 16:
                    mid = part.shape[0] // 2
                    part = part[:mid] + part[mid:]
                cols_ref[pl.ds(w, 1)] += jnp.sum(part.astype(F32), axis=0, keepdims=True)

            in_groups(lists_ref[COUNTS + region], pair)
        total = cols_ref[...]
        col_lse_ref[...] = jnp.where(
            total > 0.0,
            jnp.log(jnp.maximum(total, 1e-37)) + (0.5 * log_n - 0.5 * SHIFT),
            NEVER,
        )

    @pl.when(jnp.logical_not(fine))
    def _():
        careful_cols(
            lists_ref, at_ref, b_ref, lambda s: rows_ref[s][:, 0:1], cols_ref, col_lse_ref
        )


def lse_of(values):
    top = functools.reduce(jnp.maximum, values)
    return top + jnp.log(sum(jnp.exp(v - top) for v in values))


def exchange_kernel(
    log_n, first_ref, second_ref, g_ref, total_ref,
    to_left, to_right, from_left, from_right, from_left2, from_right2, send_sems, receive_sems,
):
    blocks = total_ref.shape[0]
    devices = lax.axis_size("cells")
    here = lax.axis_index("cells")
    peers = [lax.rem(here + devices + step, devices) for step in (-1, 1, -2, 2)]
    barrier = pltpu.get_barrier_semaphore()
    for peer in peers:
        pl.semaphore_signal(
            barrier, inc=1, device_id=(peer,), device_id_type=pl.DeviceIdType.MESH
        )
    to_left[pl.ds(0, 2 * blocks)] = first_ref[pl.ds(0, 2 * blocks)]
    to_left[pl.ds(2 * blocks, blocks)] = second_ref[pl.ds(0, blocks)]
    to_right[pl.ds(0, 2 * blocks)] = first_ref[pl.ds(blocks, 2 * blocks)]
    to_right[pl.ds(2 * blocks, blocks)] = second_ref[pl.ds(2 * blocks, blocks)]
    pl.semaphore_wait(barrier, len(peers))
    copies = []
    for i, (given, taken) in enumerate((
        (to_left, from_right),
        (to_right, from_left),
        (to_left.at[pl.ds(0, blocks)], from_right2),
        (to_right.at[pl.ds(blocks, blocks)], from_left2),
    )):
        copy = pltpu.make_async_remote_copy(
            src_ref=given,
            dst_ref=taken,
            send_sem=send_sems.at[i],
            recv_sem=receive_sems.at[i],
            device_id=(peers[i],),
            device_id_type=pl.DeviceIdType.MESH,
        )
        copy.start()
        copies.append(copy)
    for copy in copies:
        copy.wait()
    low, own, high = (pl.ds(i * blocks, blocks) for i in range(3))
    total_ref[...] = lse_of([second_ref[own], from_right[high], from_left[high]])
    g_ref[...] = jnp.zeros(g_ref.shape, F32)
    for place, values in (
        (low, [first_ref[low], from_left[low], from_left2[...]]),
        (own, [first_ref[own], from_right[low], from_left[own]]),
        (high, [first_ref[high], from_right[own], from_right2[...]]),
    ):
        g_ref[place] = 0.5 * (log_n - lse_of(values))


def row_kernel(
    log_n,
    at_ref, lists_ref, b_ref, top_ref, k_ref, row_lse_ref, g_ref, total_ref, rows_in,
    source_ref, target_ref, rows_ref, second_ref, sums_ref, v_ref,
):
    blocks = source_ref.shape[0]
    target_ref[...] = (0.5 * entropy) * (g_ref[pl.ds(blocks, blocks)] + log_n - total_ref[...])
    g = g_ref[...]
    fine = within(top_ref) & (jnp.max(g) <= 60.0) & (jnp.min(g) >= 0.0)

    @pl.when(fine)
    def _():
        g_line = jnp.exp(g_ref[...] - G_SHIFT)
        for w in range(g_line.shape[0]):
            v_ref[w] = jnp.broadcast_to(g_line[w : w + 1], v_ref.shape[1:]).astype(BF16)

        def start(s, carry):
            sums_ref[s] = jnp.zeros(sums_ref.shape[1:], BF16)
            return carry

        lax.fori_loop(0, blocks, start, 0, unroll=8)
        for region in range(3):
            base = base_of(lists_ref, region)

            def pair(at, region=region, base=base):
                s, w = entry(lists_ref, region * REGION + at)
                line = v_ref[w]
                held = k_ref[base + at]
                part = held.reshape(-1, *line.shape) * line[None]
                part = part.reshape(held.shape)
                sums_ref[s] += part[:, :128] + part[:, 128:]

            in_groups(lists_ref[COUNTS + region], pair)
        wide = (8 * 128, 128)
        group = lax.shift_right_logical(lax.broadcasted_iota(jnp.int32, wide, 0), 7)
        lane = lax.broadcasted_iota(jnp.int32, wide, 1)
        sums = None
        for first in range(0, blocks, 8):
            parts = jnp.concatenate([sums_ref[first + i] for i in range(8)], axis=1)
            pick = jnp.where(lane == group + first, 1.0, 0.0).astype(BF16)
            part = jnp.dot(parts, pick, preferred_element_type=F32)
            sums = part if sums is None else sums + part
        second_ref[...] = jnp.log(sums.T[:blocks]) - SHIFT + G_SHIFT

    @pl.when(jnp.logical_not(fine))
    def _():
        careful_rows(
            lists_ref, at_ref, b_ref, rows_ref, lambda w: g_ref[pl.ds(w, 1)], second_ref, log_n
        )

    first = 0.5 * (log_n - row_lse_ref[...])
    source_ref[...] = (0.5 * entropy) * (first + log_n - second_ref[...])


def in_hbm(array):
    return pltpu.with_memory_space_constraint(array, pltpu.HBM)


def on_device(source_cells, target_cells, partners, home):
    blocks, _, cells = source_cells.shape
    source_cells = source_cells.transpose(1, 0, 2)
    target_cells = target_cells.transpose(1, 0, 2)
    stage = pltpu.VMEM(source_cells.shape, BF16)
    wide = pltpu.VMEM((2, 56 * blocks, 128), F32)
    links = partners.shape[1]
    devices = lax.axis_size("cells")
    log_n = math.log(blocks * devices * cells)
    window = 128
    places = blocks * links + 3 * (WAYS - 1)

    def moved(block, step):
        return lax.ppermute(block, "cells", [(i, step(i) % devices) for i in range(devices)])

    far = moved(target_cells, lambda i: i + 1 if i % 2 else i - 1)
    sibling = in_hbm(moved(target_cells, lambda i: i ^ 1))

    vm = lambda shape, dtype: pltpu.VMEM(shape, dtype)
    at_s = vm((blocks, cells, DEPTH), BF16)
    b_s = vm((3 * blocks + 1, DEPTH, cells), BF16)
    top_s = vm((8, cells), F32)
    k_s = vm((places, cells, cells), BF16)
    rows_s = vm((blocks, cells, 128), F32)
    cols_s = vm((window, cells), F32)
    u_s = vm((blocks, cells, 128), BF16)
    lines_s = vm((blocks, cells), F32)
    limit = pltpu.CompilerParams(vmem_limit_bytes=8 * 2**20)

    at, b, lists, top = pl.pallas_call(
        prepare_kernel,
        out_shape=[at_s, b_s, pltpu.SMEM((COUNTS + 16,), jnp.int32), top_s],
        in_specs=[HBM] * 4,
        out_specs=[VMEM, VMEM, SMEM, VMEM],
        scratch_shapes=[
            stage, stage, pltpu.SMEM((links, blocks), jnp.int32), pltpu.SMEM(home.shape, jnp.int32),
            pltpu.SemaphoreType.DMA((4,)), wide, wide,
        ],
        compiler_params=limit,
        name="prepare",
    )(*map(in_hbm, (source_cells, target_cells, partners.T, home)))
    b, top, k, rows, cols = pl.pallas_call(
        near_kernel,
        out_shape=[b_s, top_s, k_s, rows_s, cols_s],
        in_specs=[HBM, VMEM, SMEM, VMEM, VMEM],
        out_specs=[VMEM] * 5,
        input_output_aliases={3: 0, 4: 1},
        scratch_shapes=[stage, pltpu.SemaphoreType.DMA, wide],
        compiler_params=limit,
        name="near_pairs",
    )(sibling, at, lists, b, top)
    b, top, k, rows, cols, u, row_lse, col_lse = pl.pallas_call(
        functools.partial(far_kernel, log_n),
        out_shape=[b_s, top_s, k_s, rows_s, cols_s, u_s, lines_s, cols_s],
        in_specs=[VMEM, VMEM, SMEM] + [VMEM] * 5,
        out_specs=[VMEM] * 8,
        input_output_aliases={3: 0, 4: 1, 5: 2, 6: 3, 7: 4},
        scratch_shapes=[wide],
        compiler_params=limit,
        name="far_pairs",
    )(far, at, lists, b, top, k, rows, cols)

    col_lse2, _ = pl.pallas_call(
        functools.partial(column_kernel, log_n),
        out_shape=[cols_s, cols_s],
        in_specs=[VMEM, SMEM] + [VMEM] * 5,
        out_specs=[VMEM] * 2,
        compiler_params=limit,
        name="second_columns",
    )(at, lists, b, top, k, rows, u)
    result = jax.ShapeDtypeStruct((blocks, cells), F32)
    message = pltpu.VMEM((3 * blocks, cells), F32)
    block = pltpu.VMEM((blocks, cells), F32)
    g, total = pl.pallas_call(
        functools.partial(exchange_kernel, log_n),
        out_shape=[cols_s, lines_s],
        in_specs=[VMEM] * 2,
        out_specs=[VMEM] * 2,
        scratch_shapes=[message] * 4 + [block] * 2 + [pltpu.SemaphoreType.DMA((4,))] * 2,
        compiler_params=pltpu.CompilerParams(
            vmem_limit_bytes=8 * 2**20, collective_id=0, has_side_effects=True
        ),
        name="exchange",
    )(col_lse, col_lse2)
    source_pot, target_pot, *_ = pl.pallas_call(
        functools.partial(row_kernel, log_n),
        out_shape=[result, result, rows_s, lines_s, u_s],
        in_specs=[VMEM, SMEM] + [VMEM] * 7,
        out_specs=[VMEM] * 5,
        input_output_aliases={8: 2},
        scratch_shapes=[pltpu.VMEM((window, 16, cells), BF16)],
        compiler_params=limit,
        name="second_rows",
    )(at, lists, b, top, k, row_lse, g, total, rows)
    return source_pot, target_pot


def solution(mesh):
    in_specs = (P("cells", None, None), P("cells", None, None), P("cells", None), P())
    out_specs = (P("cells", None), P("cells", None))
    return jax.shard_map(
        on_device, mesh=mesh, in_specs=in_specs, out_specs=out_specs, check_vma=False
    )
```
